32 devices in a mesh: sec: 4 (over x, core), blk: 4 (over z), aux: 2 (over y).
Axes of the slice: x: 2, y: 2, z: 4, core: 2. Of those that a mesh axis runs over, the one named last changes fastest.
Arguments:
- half_ints: bfloat16 [16, 2048, 1024], P('blk', 'aux', 'sec'), may hold values from -0.59765625 to 0.59765625
- coeffs: bfloat16 [1024, 1024], replicated, may hold values from -0.1875 to 0.1875
- occ_energy: float32 [16], replicated, may hold values from -1.5 to -0.3
- vir_energy: float32 [1024], replicated, may hold values from 0.2 to 3
Outputs:
- back_density: float32 [1024, 16, 2048], P('sec', 'blk', 'aux')
The draws below stay inside these ranges and needn't reach their ends.
All inputs are finite; a program needn't handle non-finite values.
Results may differ from the reference program's by a relative error of at most 0.003.
Values may be sent and summed in bfloat16 or wider, within the bound.
A program may use at most 128 MiB of HBM per device.

```python
import jax
import jax.numpy as jnp
from jax import lax

NOCC = 16
NVIR = 1024
NAUX = 2048
NBAS = 1024


def levels(own_key, dims, shards, least, largest):
    def one(position, parts):
        draws = jax.random.uniform(jax.random.fold_in(jax.random.fold_in(own_key, 6), position), (parts,), jnp.float32, least / len(shards), largest / len(shards))
        return jnp.repeat(jnp.exp(draws), dims[position] // parts).reshape((-1,) + (1,) * (len(dims) - position - 1))

    loudness = one(*shards[0])
    for cut in shards[1:]:
        loudness = loudness * one(*cut)
    return loudness


def gaussian(key, shape, width, limit, split=(), kind=jnp.bfloat16):
    loudness = levels(key, shape, split, -0.22, 0.18) if split else 1.0
    array = jax.random.normal(key, shape, jnp.float32) * width * loudness
    return jnp.minimum(jnp.maximum(array, -limit), limit).astype(kind)


def setup_inputs(seed: int = 0) -> dict:
    splits = jax.random.split(jax.random.key(seed), 5)
    return {
        "half_ints": gaussian(splits[0], (NOCC, NAUX, NBAS), 0.1, 0.59765625, ((0, 4), (1, 2), (2, 4))),
        "coeffs": gaussian(splits[1], (NBAS, NVIR), NBAS ** -0.5, 0.1875),
        "occ_energy": jnp.clip(jax.random.uniform(splits[2], (NOCC,), jnp.float32, -1.5, -0.3), -1.5, -0.3),
        "vir_energy": jnp.clip(jax.random.uniform(splits[3], (NVIR,), jnp.float32, 0.2, 3.0), 0.2, 3.0),
    }


def reference(half_ints, coeffs, occ_energy, vir_energy):
    high = lax.Precision.HIGHEST
    transformed = jnp.einsum("ipm,ma->ipa", half_ints.astype(jnp.float32), coeffs.astype(jnp.float32), precision=high).astype(jnp.bfloat16)
    trans_wide = lax.optimization_barrier(transformed).astype(jnp.float32)

    def per_occupied(index):
        own_rows = lax.dynamic_index_in_dim(trans_wide, index, 0, keepdims=False)
        tiles = jnp.einsum("pa,jpb->jab", own_rows, trans_wide, precision=high)
        own_energy = lax.dynamic_index_in_dim(occ_energy, index, 0, keepdims=False)
        denominator = own_energy + occ_energy[:, None, None] - vir_energy[None, :, None] - vir_energy[None, None, :]
        amplitude = (1.3 * tiles / denominator).astype(jnp.bfloat16)
        amplitude = lax.optimization_barrier(amplitude).astype(jnp.float32)
        return jnp.einsum("jab,jpb->pa", amplitude, trans_wide, precision=high)

    density = lax.map(per_occupied, jnp.arange(NOCC, dtype=jnp.int32))
    density_half = lax.optimization_barrier(density.astype(jnp.bfloat16)).astype(jnp.float32)
    return jnp.einsum("ma,ipa->mip", coeffs.astype(jnp.float32), density_half, precision=high)
```

```python
import jax
import jax.numpy as jnp
from jax import lax
from jax.sharding import PartitionSpec as P

CORES = 2


def shards(half_ints, coeffs, occ_energy, vir_energy):
    sec_size, blk_size, aux_size = (lax.axis_size(n) for n in ("sec", "blk", "aux"))
    sec_index, blk_index, aux_index = (lax.axis_index(n) for n in ("sec", "blk", "aux"))
    cores = CORES if sec_size % CORES == 0 else 1
    xs = sec_size // cores
    x_index, core_index = sec_index // cores, sec_index % cores
    occ_block, aux_half, basis_slice = half_ints.shape
    vir_total = coeffs.shape[1]
    vir_part = vir_total // cores
    key_width = vir_part // (xs * aux_size)
    quarter = aux_half // xs
    aux_total = aux_half * aux_size

    def plane_shift(v, s, t):
        perm = []
        for i in range(sec_size):
            for j in range(aux_size):
                to = ((i // cores + s) % xs) * cores + i % cores
                perm.append((i * aux_size + j, to * aux_size + (j + t) % aux_size))
        return lax.ppermute(v, ("sec", "aux"), perm)

    def core_shift(v, k):
        perm = [(i, i // cores * cores + (i + k) % cores) for i in range(sec_size)]
        return lax.ppermute(v, "sec", perm)

    def gathered_cores(v, axis):
        return jnp.concatenate([v] + [core_shift(v, k) for k in range(1, cores)], axis)

    def line(v, by):
        perm = [(i, i + by) for i in range(blk_size) if 0 <= i + by < blk_size]
        return lax.ppermute(v, "blk", perm)

    pieces = []
    for s in range(xs):
        start = ((x_index + s) % xs) * quarter
        part = lax.dynamic_slice_in_dim(half_ints, start, quarter, 1)
        pieces.append(plane_shift(part, s, 0) if s else part)
    rows = gathered_cores(jnp.concatenate(pieces, 2), 2)
    own_columns = lax.dynamic_slice_in_dim(coeffs, core_index * vir_part, vir_part, 1)
    blocks = []
    for k in range(cores):
        for s in range(xs):
            source = ((x_index - s) % xs) * cores + (core_index - k) % cores
            blocks.append(lax.dynamic_slice_in_dim(own_columns, source * basis_slice, basis_slice, 0))
    transformed = jnp.einsum(
        "ipm,ma->ipa", rows, jnp.concatenate(blocks, 0), preferred_element_type=jnp.float32
    ).astype(jnp.bfloat16)

    def key_columns(s, t):
        group = ((x_index + s) % xs) * aux_size + (aux_index + t) % aux_size
        return lax.dynamic_slice_in_dim(transformed, group * key_width, key_width, 2)

    turns = [(t, s) for t in range(aux_size) for s in range(xs)]
    keys = [plane_shift(key_columns(s, t), s, t) if s or t else key_columns(0, 0) for t, s in turns]
    own_keys = jnp.concatenate(keys, 1)
    transformed, own_keys = lax.optimization_barrier((transformed, own_keys))
    queries = jnp.concatenate(
        [plane_shift(transformed, s, t) if s or t else transformed for t, s in turns], 1
    )

    up, down = [own_keys], [own_keys]
    for _ in range(blk_size - 1):
        up.append(line(up[-1], 1))
        down.append(line(down[-1], -1))

    def arrival(z, stage):
        others = sorted((b for b in range(blk_size)), key=lambda b: (abs(b - z), b))
        return others[stage]

    own_energy = lax.dynamic_slice_in_dim(occ_energy, blk_index * occ_block, occ_block)
    own_virtual = lax.dynamic_slice_in_dim(vir_energy, core_index * vir_part, vir_part)
    group = x_index * aux_size + aux_index
    key_virtual = jnp.concatenate([
        lax.dynamic_slice_in_dim(
            vir_energy, (core_index - k) % cores * vir_part + group * key_width, key_width
        )
        for k in range(cores)
    ])

    def stage_keys(stage):
        choices = {}
        for z in range(blk_size):
            b = arrival(z, stage)
            choices.setdefault(b - z, []).append(z)
        chosen = None
        for offset, planes in choices.items():
            block = down[offset] if offset > 0 else up[-offset]
            if chosen is None:
                chosen = block
            else:
                here = jnp.any(blk_index == jnp.array(planes))
                chosen = jnp.where(here, block, chosen)
        source = jnp.array([arrival(z, stage) for z in range(blk_size)])[blk_index]
        energy = lax.dynamic_slice_in_dim(occ_energy, source * occ_block, occ_block)
        return gathered_cores(chosen, 2), energy

    def pair_step(rows, energy_rows, visiting, visit_energy):
        tiles = jnp.einsum("ipa,jpb->iajb", rows, visiting, preferred_element_type=jnp.float32)
        denominator = (
            energy_rows[:, None, None, None]
            + visit_energy[None, None, :, None]
            - own_virtual[None, :, None, None]
            - key_virtual[None, None, None, :]
        )
        amplitude = (1.3 * tiles / denominator).astype(jnp.bfloat16)
        return jnp.einsum("iajb,jpb->ipa", amplitude, visiting, preferred_element_type=jnp.float32)

    totals = None
    for stage in range(blk_size - 1):
        visiting, visit_energy = stage_keys(stage)
        if totals is not None:
            totals, visiting = lax.optimization_barrier((totals, visiting))
        term = pair_step(queries, own_energy, visiting, visit_energy)
        totals = term if totals is None else totals + term
    visiting, visit_energy = stage_keys(blk_size - 1)
    wide = []
    for i in range(occ_block):
        part = pair_step(queries[i : i + 1], own_energy[i : i + 1], visiting, visit_energy)[0]
        if totals is not None:
            part = part + totals[i]
        part = part.reshape(aux_size, xs, quarter, vir_part)
        half = part[0]
        for t in range(1, aux_size):
            half = half + plane_shift(part[(-t) % aux_size].astype(jnp.bfloat16), 0, t)
        total = half
        for s in range(1, xs):
            received = plane_shift(half.astype(jnp.bfloat16), s, 0)
            total = total + jnp.roll(received, s, 0)
        whole = gathered_cores(total.astype(jnp.bfloat16), 2)
        wide.append(whole)
    wide = jnp.stack(wide)
    wide = jnp.concatenate(
        [lax.dynamic_slice_in_dim(wide, (x_index - p) % xs, 1, 1)[:, 0] for p in range(xs)], 1
    )
    coeff_rows = lax.dynamic_slice_in_dim(coeffs, sec_index * basis_slice, basis_slice, 0)
    coeff_rows = jnp.concatenate([
        lax.dynamic_slice_in_dim(coeff_rows, (core_index - k) % cores * vir_part, vir_part, 1)
        for k in range(cores)
    ], 1)
    return jnp.einsum("ma,ipa->mip", coeff_rows, wide, preferred_element_type=jnp.float32)


def solution(mesh):
    placed = (P("blk", "aux", "sec"), P(), P(), P())
    return jax.shard_map(
        shards, mesh=mesh, in_specs=placed, out_specs=P("sec", "blk", "aux"), check_vma=False
    )
```

```python
import jax
import jax.numpy as jnp
from jax import lax
from jax.sharding import PartitionSpec as P

CORES = 2


def shards(half_ints, coeffs, occ_energy, vir_energy):
    sec_size, blk_size, aux_size = (lax.axis_size(n) for n in ("sec", "blk", "aux"))
    sec_index, blk_index, aux_index = (lax.axis_index(n) for n in ("sec", "blk", "aux"))
    cores = CORES if sec_size % CORES == 0 else 1
    xs = sec_size // cores
    x_index, core_index = sec_index // cores, sec_index % cores
    occ_block, aux_half, basis_slice = half_ints.shape
    vir_total = coeffs.shape[1]
    vir_part = vir_total // cores
    key_width = vir_part // (xs * aux_size)
    quarter = aux_half // xs
    aux_total = aux_half * aux_size

    def plane_shift(v, s, t):
        perm = []
        for i in range(sec_size):
            for j in range(aux_size):
                to = ((i // cores + s) % xs) * cores + i % cores
                perm.append((i * aux_size + j, to * aux_size + (j + t) % aux_size))
        return lax.ppermute(v, ("sec", "aux"), perm)

    def core_shift(v, k):
        perm = [(i, i // cores * cores + (i + k) % cores) for i in range(sec_size)]
        return lax.ppermute(v, "sec", perm)

    def gathered_cores(v, axis):
        return jnp.concatenate([v] + [core_shift(v, k) for k in range(1, cores)], axis)

    def line(v, by):
        perm = [(i, i + by) for i in range(blk_size) if 0 <= i + by < blk_size]
        return lax.ppermute(v, "blk", perm)

    pieces = []
    for s in range(xs):
        start = ((x_index + s) % xs) * quarter
        part = lax.dynamic_slice_in_dim(half_ints, start, quarter, 1)
        pieces.append(plane_shift(part, s, 0) if s else part)
    rows = gathered_cores(jnp.concatenate(pieces, 2), 2)
    own_columns = lax.dynamic_slice_in_dim(coeffs, core_index * vir_part, vir_part, 1)
    blocks = []
    for k in range(cores):
        for s in range(xs):
            source = ((x_index - s) % xs) * cores + (core_index - k) % cores
            blocks.append(lax.dynamic_slice_in_dim(own_columns, source * basis_slice, basis_slice, 0))
    transformed = jnp.einsum(
        "ipm,ma->ipa", rows, jnp.concatenate(blocks, 0), preferred_element_type=jnp.float32
    ).astype(jnp.bfloat16)

    def key_columns(s, t):
        group = ((x_index + s) % xs) * aux_size + (aux_index + t) % aux_size
        return lax.dynamic_slice_in_dim(transformed, group * key_width, key_width, 2)

    turns = [(t, s) for t in range(aux_size) for s in range(xs)]
    keys = [plane_shift(key_columns(s, t), s, t) if s or t else key_columns(0, 0) for t, s in turns]
    own_keys = jnp.concatenate(keys, 1)
    transformed, own_keys = lax.optimization_barrier((transformed, own_keys))
    near = {(t, s): plane_shift(transformed, s, t) for t, s in turns if (s == 0) != (t == 0)}
    far_turns = [(t, s) for t, s in turns if s and t]
    far = {}

    up, down = [own_keys], [own_keys]
    for step in range(1, blk_size):
        before = (up[-1], down[-1])
        if step == 2:
            before, near = lax.optimization_barrier((before, near))
        if step == 3:
            before, far = lax.optimization_barrier((before, far))
        up.append(line(before[0], 1))
        down.append(line(before[1], -1))
        if step == 2:
            far = {(t, s): plane_shift(transformed, s, t) for t, s in far_turns}
    if blk_size < 3:
        far = {(t, s): plane_shift(transformed, s, t) for t, s in far_turns}
    held = {(0, 0): transformed, **near, **far}
    queries = jnp.concatenate([held[turn] for turn in turns], 1)

    def arrival(z, stage):
        others = sorted((b for b in range(blk_size)), key=lambda b: (abs(b - z), b))
        return others[stage]

    own_energy = lax.dynamic_slice_in_dim(occ_energy, blk_index * occ_block, occ_block)
    own_virtual = lax.dynamic_slice_in_dim(vir_energy, core_index * vir_part, vir_part)
    group = x_index * aux_size + aux_index
    key_virtual = jnp.concatenate([
        lax.dynamic_slice_in_dim(
            vir_energy, (core_index - k) % cores * vir_part + group * key_width, key_width
        )
        for k in range(cores)
    ])

    def stage_keys(stage):
        choices = {}
        for z in range(blk_size):
            b = arrival(z, stage)
            choices.setdefault(b - z, []).append(z)
        chosen = None
        for offset, planes in choices.items():
            block = down[offset] if offset > 0 else up[-offset]
            if chosen is None:
                chosen = block
            else:
                here = jnp.any(blk_index == jnp.array(planes))
                chosen = jnp.where(here, block, chosen)
        source = jnp.array([arrival(z, stage) for z in range(blk_size)])[blk_index]
        energy = lax.dynamic_slice_in_dim(occ_energy, source * occ_block, occ_block)
        return gathered_cores(chosen, 2), energy

    def amplitudes(rows, energy_rows, visiting, visit_energy):
        tiles = jnp.einsum("ipa,jpb->iajb", rows, visiting, preferred_element_type=jnp.float32)
        denominator = (
            energy_rows[:, None, None, None]
            + visit_energy[None, None, :, None]
            - own_virtual[None, :, None, None]
            - key_virtual[None, None, None, :]
        )
        return (1.3 * tiles / denominator).astype(jnp.bfloat16)

    def contracted(amplitude, visiting):
        return jnp.einsum("ajb,jpb->pa", amplitude, visiting, preferred_element_type=jnp.float32)

    early = [stage_keys(stage) for stage in range(blk_size - 1)]
    early_amplitude = None
    if early:
        early_keys = jnp.concatenate([k for k, _ in early], 0)
        early_energy = jnp.concatenate([e for _, e in early], 0)
        early_amplitude = amplitudes(queries, own_energy, early_keys, early_energy)
    visiting, visit_energy = stage_keys(blk_size - 1)
    parts, wide = [], []
    for i in range(occ_block):
        rows, before = queries[i : i + 1], None if early_amplitude is None else early_amplitude[i]
        if parts:
            rows, before, parts[-1] = lax.optimization_barrier((rows, before, parts[-1]))
        part = contracted(amplitudes(rows, own_energy[i : i + 1], visiting, visit_energy)[0], visiting)
        if before is not None:
            part = part + contracted(before, early_keys)
        part = part.reshape(aux_size, xs, quarter, vir_part)
        away = [plane_shift(part[(-t) % aux_size].astype(jnp.bfloat16), 0, t) for t in range(1, aux_size)]
        parts.append(part[0])
        wide.append(away)
    for i in range(occ_block):
        half = parts[i]
        for received in wide[i]:
            half = half + received
        total = half
        for s in range(1, xs):
            received = plane_shift(half.astype(jnp.bfloat16), s, 0)
            total = total + jnp.roll(received, s, 0)
        wide[i] = gathered_cores(total.astype(jnp.bfloat16), 2)
    wide = jnp.stack(wide)
    wide = jnp.concatenate(
        [lax.dynamic_slice_in_dim(wide, (x_index - p) % xs, 1, 1)[:, 0] for p in range(xs)], 1
    )
    coeff_rows = lax.dynamic_slice_in_dim(coeffs, sec_index * basis_slice, basis_slice, 0)
    coeff_rows = jnp.concatenate([
        lax.dynamic_slice_in_dim(coeff_rows, (core_index - k) % cores * vir_part, vir_part, 1)
        for k in range(cores)
    ], 1)
    return jnp.einsum("ma,ipa->mip", coeff_rows, wide, preferred_element_type=jnp.float32)


def solution(mesh):
    placed = (P("blk", "aux", "sec"), P(), P(), P())
    return jax.shard_map(
        shards, mesh=mesh, in_specs=placed, out_specs=P("sec", "blk", "aux"), check_vma=False
    )
```

```python
import jax
import jax.numpy as jnp
from jax import lax
from jax.sharding import PartitionSpec as P

CORES = 2


def shards(half_ints, coeffs, occ_energy, vir_energy):
    sec_size, blk_size, aux_size = (lax.axis_size(n) for n in ("sec", "blk", "aux"))
    sec_index, blk_index, aux_index = (lax.axis_index(n) for n in ("sec", "blk", "aux"))
    cores = CORES if sec_size % CORES == 0 else 1
    xs = sec_size // cores
    x_index, core_index = sec_index // cores, sec_index % cores
    occ_block, aux_half, basis_slice = half_ints.shape
    vir_total = coeffs.shape[1]
    vir_part = vir_total // cores
    key_width = vir_part // (xs * aux_size)
    quarter = aux_half // xs
    aux_total = aux_half * aux_size

    def plane_shift(v, s, t):
        perm = []
        for i in range(sec_size):
            for j in range(aux_size):
                to = ((i // cores + s) % xs) * cores + i % cores
                perm.append((i * aux_size + j, to * aux_size + (j + t) % aux_size))
        return lax.ppermute(v, ("sec", "aux"), perm)

    def core_shift(v, k):
        perm = [(i, i // cores * cores + (i + k) % cores) for i in range(sec_size)]
        return lax.ppermute(v, "sec", perm)

    def gathered_cores(v, axis):
        return jnp.concatenate([v] + [core_shift(v, k) for k in range(1, cores)], axis)

    def line(v, by):
        perm = [(i, i + by) for i in range(blk_size) if 0 <= i + by < blk_size]
        return lax.ppermute(v, "blk", perm)

    pieces = []
    for s in range(xs):
        start = ((x_index + s) % xs) * quarter
        part = lax.dynamic_slice_in_dim(half_ints, start, quarter, 1)
        pieces.append(plane_shift(part, s, 0) if s else part)
    rows = gathered_cores(jnp.concatenate(pieces, 2), 2)
    own_columns = lax.dynamic_slice_in_dim(coeffs, core_index * vir_part, vir_part, 1)
    blocks = []
    for k in range(cores):
        for s in range(xs):
            source = ((x_index - s) % xs) * cores + (core_index - k) % cores
            blocks.append(lax.dynamic_slice_in_dim(own_columns, source * basis_slice, basis_slice, 0))
    transformed = jnp.einsum(
        "ipm,ma->ipa", rows, jnp.concatenate(blocks, 0), preferred_element_type=jnp.float32
    ).astype(jnp.bfloat16)

    def key_columns(s, t):
        group = ((x_index + s) % xs) * aux_size + (aux_index + t) % aux_size
        return lax.dynamic_slice_in_dim(transformed, group * key_width, key_width, 2)

    turns = [(t, s) for t in range(aux_size) for s in range(xs)]
    keys = [plane_shift(key_columns(s, t), s, t) if s or t else key_columns(0, 0) for t, s in turns]
    own_keys = jnp.concatenate(keys, 1)
    transformed, own_keys = lax.optimization_barrier((transformed, own_keys))
    near = {(t, s): plane_shift(transformed, s, t) for t, s in turns if (s == 0) != (t == 0)}
    far_turns = [(t, s) for t, s in turns if s and t]
    far = {}

    up, down = [own_keys], [own_keys]
    for step in range(1, blk_size):
        before = (up[-1], down[-1])
        if step == 2:
            before, near = lax.optimization_barrier((before, near))
        if step == 3:
            before, far = lax.optimization_barrier((before, far))
        up.append(line(before[0], 1))
        down.append(line(before[1], -1))
        if step == 2:
            far = {(t, s): plane_shift(transformed, s, t) for t, s in far_turns}
    if blk_size < 3:
        far = {(t, s): plane_shift(transformed, s, t) for t, s in far_turns}
    held = {(0, 0): transformed, **near, **far}
    queries = jnp.concatenate([held[turn] for turn in turns], 1)

    def arrival(z, stage):
        others = sorted((b for b in range(blk_size)), key=lambda b: (abs(b - z), b))
        return others[stage]

    own_energy = lax.dynamic_slice_in_dim(occ_energy, blk_index * occ_block, occ_block)
    own_virtual = lax.dynamic_slice_in_dim(vir_energy, core_index * vir_part, vir_part)
    group = x_index * aux_size + aux_index
    key_virtual = jnp.concatenate([
        lax.dynamic_slice_in_dim(
            vir_energy, (core_index - k) % cores * vir_part + group * key_width, key_width
        )
        for k in range(cores)
    ])

    def stage_keys(stage):
        choices = {}
        for z in range(blk_size):
            b = arrival(z, stage)
            choices.setdefault(b - z, []).append(z)
        chosen = None
        for offset, planes in choices.items():
            block = down[offset] if offset > 0 else up[-offset]
            if chosen is None:
                chosen = block
            else:
                here = jnp.any(blk_index == jnp.array(planes))
                chosen = jnp.where(here, block, chosen)
        source = jnp.array([arrival(z, stage) for z in range(blk_size)])[blk_index]
        energy = lax.dynamic_slice_in_dim(occ_energy, source * occ_block, occ_block)
        return gathered_cores(chosen, 2), energy

    def amplitudes(rows, energy_rows, visiting, visit_energy):
        tiles = jnp.einsum("ipa,jpb->iajb", rows, visiting, preferred_element_type=jnp.float32)
        denominator = (
            energy_rows[:, None, None, None]
            + visit_energy[None, None, :, None]
            - own_virtual[None, :, None, None]
            - key_virtual[None, None, None, :]
        )
        return (1.3 * tiles / denominator).astype(jnp.bfloat16)

    def contracted(amplitude, visiting):
        return jnp.einsum("ajb,jpb->pa", amplitude, visiting, preferred_element_type=jnp.float32)

    early = [stage_keys(stage) for stage in range(blk_size - 1)]
    early_amplitude = None
    if early:
        early_keys = jnp.concatenate([k for k, _ in early], 0)
        early_energy = jnp.concatenate([e for _, e in early], 0)
        early_amplitude = amplitudes(queries, own_energy, early_keys, early_energy)
        up[-1], down[-1], early_amplitude = lax.optimization_barrier((up[-1], down[-1], early_amplitude))
    visiting, visit_energy = stage_keys(blk_size - 1)
    parts, wide = [], []
    for i in range(occ_block):
        rows, before = queries[i : i + 1], None if early_amplitude is None else early_amplitude[i]
        if parts:
            rows, before, parts[-1] = lax.optimization_barrier((rows, before, parts[-1]))
        if i > 1:
            rows, before, wide[i - 2] = lax.optimization_barrier((rows, before, wide[i - 2]))
        part = contracted(amplitudes(rows, own_energy[i : i + 1], visiting, visit_energy)[0], visiting)
        if before is not None:
            part = part + contracted(before, early_keys)
        part = part.reshape(aux_size, xs, quarter, vir_part)
        away = [plane_shift(part[(-t) % aux_size].astype(jnp.bfloat16), 0, t) for t in range(1, aux_size)]
        parts.append(part[0])
        wide.append(away)
    for i in range(occ_block):
        half = parts[i]
        for received in wide[i]:
            half = half + received
        total = half
        for s in range(1, xs):
            received = plane_shift(half.astype(jnp.bfloat16), s, 0)
            total = total + jnp.roll(received, s, 0)
        wide[i] = gathered_cores(total.astype(jnp.bfloat16), 2)
    wide = jnp.stack(wide)
    wide = jnp.concatenate(
        [lax.dynamic_slice_in_dim(wide, (x_index - p) % xs, 1, 1)[:, 0] for p in range(xs)], 1
    )
    coeff_rows = lax.dynamic_slice_in_dim(coeffs, sec_index * basis_slice, basis_slice, 0)
    coeff_rows = jnp.concatenate([
        lax.dynamic_slice_in_dim(coeff_rows, (core_index - k) % cores * vir_part, vir_part, 1)
        for k in range(cores)
    ], 1)
    return jnp.einsum("ma,ipa->mip", coeff_rows, wide, preferred_element_type=jnp.float32)


def solution(mesh):
    placed = (P("blk", "aux", "sec"), P(), P(), P())
    return jax.shard_map(
        shards, mesh=mesh, in_specs=placed, out_specs=P("sec", "blk", "aux"), check_vma=False
    )
```
